32 devices in a mesh: learn: 4 (over y, x), act: 8 (over z, core).
Axes of the slice: x: 2, y: 2, z: 4, core: 2. Of those that a mesh axis runs over, the one named last changes fastest.
Arguments:
- positions: int32 [2, 32, 361], P(None, ('learn', 'act')), may hold values from 0 to 2
- to_move: int32 [2, 32], P(None, ('learn', 'act')), may hold values from 0 to 1
- legal_moves: int32 [2, 32, 361], P(None, ('learn', 'act')), may hold values 0 or 1
- master: float32 [4, 2, 2304, 256], P('learn', None, 'act'), may hold values from -0.125 to 0.125
- gradients: float32 [4, 4, 2, 2304, 256], P('learn', None, None, 'act'), may hold values from -0.4375 to 0.4375
- stem_weight: bfloat16 [36, 256], replicated, may hold values from -1 to 1
- policy_weight: float32 [256], replicated, may hold values from -2 to 2
- pass_weight: float32 [256], replicated, may hold values from -2 to 2
- value_weight: float32 [256], replicated, may hold values from -0.375 to 0.375
Outputs:
- updated: float32 [4, 2, 2304, 256], P('learn', None, 'act')
- policy_logp: float32 [2, 32, 362], P(None, ('learn', 'act'))
- value: float32 [2, 32], P(None, ('learn', 'act'))
The draws below stay inside these ranges and needn't reach their ends.
All inputs are finite; a program needn't handle non-finite values. No bound on the sum of `legal_moves` on one device may be relied on, other than what follows from the above.
Results may differ from the reference program's by a relative error of at most 0.008.
Values may be sent and summed in bfloat16 or wider, within the bound.
No kernel may reach another device: no remote copies, remote signals or barrier semaphores. Data moves between devices by JAX's collectives and lax.ppermute only.
A program may use at most 128 MiB of HBM per device.

```python
import jax
import jax.numpy as jnp
from jax import lax

C = 256
BOARD = 19
CELLS = 361
PLANES = 4
STEPS = 2
LAYERS = 4
POSITIONS = 32
N_LEARN = 4


def touch_ends(drawn, own_key, smallest, high):
    longest = drawn.shape.index(max(drawn.shape))
    spots = []
    for shift in (0, 1):
        where = [jax.random.randint(jax.random.fold_in(own_key, axis), (), 0, length) for axis, length in enumerate(drawn.shape)]
        where[longest] = (where[longest] + shift) % drawn.shape[longest]
        spots.append(tuple(where))
    return drawn.at[spots[0]].set(smallest).at[spots[1]].set(high)


def with_spikes(entries, stream_key, source, target, parts, factor):
    def block_of(axis_at):
        return (jnp.arange(entries.shape[axis_at]) // (entries.shape[axis_at] // parts)).reshape((-1,) + (1,) * (entries.ndim - 1 - axis_at))

    near = jax.random.permutation(stream_key, parts)[block_of(target)]
    far = (block_of(target) + parts // 2) % parts
    return jnp.where((block_of(source) == near) | (block_of(source) == far), factor * entries, entries)


def level_of(stream_key, extent, cuts, low, top_value):
    level, own = 1.0, jax.random.fold_in(stream_key, 6)
    for position, parts in cuts:
        steps = jnp.exp(jax.random.uniform(jax.random.fold_in(own, position), (parts,), jnp.float32, low / len(cuts), top_value / len(cuts)))
        level = level * jnp.repeat(steps, extent[position] // parts).reshape([-1 if axis == position else 1 for axis in range(len(extent))])
    return level


def noise(key, extent, width, reach, pieces=(), kind=jnp.bfloat16):
    drawn = jax.random.normal(key, extent, jnp.float32) * width
    if len(pieces) > 0:
        drawn = level_of(key, extent, pieces, -0.22, 0.18) * drawn
    return jnp.clip(drawn, min=-reach, max=reach).astype(kind)


def heavy_noise(rng, shape, spread, limit, pieces, heavy, kind=jnp.bfloat16):
    entries = spread * jax.random.normal(rng, shape, jnp.float32)
    if pieces:
        entries = entries * level_of(rng, shape, pieces, -0.22, 0.18)
    return jnp.clip(with_spikes(entries, jax.random.fold_in(rng, 3), *heavy), -limit, limit).astype(kind)


def setup_inputs(seed: int = 0) -> dict:
    keys = jax.random.split(jax.random.key(seed), 10)
    positions = touch_ends(jax.random.randint(keys[0], (STEPS, POSITIONS, CELLS), 0, 3), jax.random.fold_in(keys[0], 1), 0, 2).astype(jnp.int32)
    to_move = touch_ends(jax.random.randint(keys[1], (STEPS, POSITIONS), 0, 2), jax.random.fold_in(keys[1], 1), 0, 1).astype(jnp.int32)
    legal_moves = touch_ends((jax.random.randint(keys[2], (STEPS, POSITIONS, CELLS), 0, 2) < 1).astype(jnp.int32), jax.random.fold_in(keys[2], 1), 0, 1)
    master = noise(keys[3], (LAYERS, 2, 9 * C, C), (9 * C) ** -0.5, 0.125, ((0, 4), (2, 8)), jnp.float32)
    gradients = heavy_noise(keys[4], (N_LEARN, LAYERS, 2, 9 * C, C), (1.0 / (9 * C) ** 0.5), 0.4375, ((0, 4), (3, 8)), (0, 1, 4, 2.0), jnp.float32)
    stem_weight = noise(keys[5], (9 * PLANES, C), (9 * PLANES) ** -0.5, 1.0)
    policy_weight = noise(keys[6], (C,), (2.0 / C ** 0.5), 2.0, (), jnp.float32)
    pass_weight = noise(keys[7], (C,), (2.0 / C ** 0.5), 2.0, (), jnp.float32)
    value_weight = noise(keys[8], (C,), C ** -0.5, 0.375, (), jnp.float32)
    return {"positions": positions, "to_move": to_move, "legal_moves": legal_moves, "master": master, "gradients": gradients, "stem_weight": stem_weight, "policy_weight": policy_weight, "pass_weight": pass_weight, "value_weight": value_weight}


def convolve(planes_in, kernel):
    padded = jnp.pad(planes_in, ((0, 0), (1, 1), (1, 1), (0, 0)))
    shifted = [padded[:, row_off:row_off + BOARD, col_off:col_off + BOARD, :] for row_off in range(3) for col_off in range(3)]
    stacked = jnp.concatenate(shifted, axis=-1)
    unrolled = stacked.reshape(-1, stacked.shape[-1])
    result = jnp.dot(unrolled, kernel, preferred_element_type=jnp.float32)
    return result.reshape(planes_in.shape[0], BOARD, BOARD, kernel.shape[1])


def make_planes(boards, sides):
    side_move = sides[:, None]
    own_stones = boards == 1 + side_move
    foe_stones = boards == 2 - side_move
    vacant = boards == 0
    filled = jnp.ones_like(own_stones)
    stacked = jnp.stack([own_stones, foe_stones, vacant, filled], axis=-1).astype(jnp.bfloat16)
    return stacked.reshape(boards.shape[0], BOARD, BOARD, PLANES)


def heads(stream, legal_rows, policy_weight, pass_weight, value_weight):
    number = stream.shape[0]
    trunk_out = jax.nn.relu(stream).reshape(number, CELLS, stream.shape[-1])
    board_raw = jnp.einsum("pcd,d->pc", trunk_out, policy_weight, precision=lax.Precision.HIGHEST)
    pooled = jnp.mean(trunk_out, axis=1)
    pass_raw = jnp.dot(pooled, pass_weight, precision=lax.Precision.HIGHEST)
    value_raw = jnp.dot(pooled, value_weight, precision=lax.Precision.HIGHEST)
    logits = 10.0 * jnp.tanh(jnp.concatenate([board_raw, pass_raw[:, None]], axis=1) / 10.0)
    allowed = jnp.concatenate([legal_rows, jnp.ones((number, 1), jnp.int32)], axis=1) > 0
    exponent = jnp.where(allowed, jnp.exp(logits), 0.0)
    denominator = jnp.sum(exponent, axis=1, keepdims=True)
    logp = jnp.where(allowed, logits - jnp.log(denominator), 0.0)
    return logp, jnp.tanh(value_raw)


def reference(positions, to_move, legal_moves, master, gradients, stem_weight, policy_weight, pass_weight, value_weight):
    gradient_sum = jnp.sum(gradients, axis=0)
    updated = master - gradient_sum / N_LEARN
    weights = updated.astype(jnp.bfloat16)
    boards = positions.reshape(-1, CELLS)
    sides = to_move.reshape(-1)
    legal_flat = legal_moves.reshape(-1, CELLS)

    def single(items):
        board_one, side_one, legal_one = items
        planes = make_planes(board_one[None], side_one[None])
        stream = convolve(planes, stem_weight)
        for layer in range(LAYERS):
            activ = jax.nn.relu(stream).astype(jnp.bfloat16)
            middle = jax.nn.relu(convolve(activ, weights[layer, 0])).astype(jnp.bfloat16)
            stream = stream + convolve(middle, weights[layer, 1])
        logp, value_one = heads(stream, legal_one[None], policy_weight, pass_weight, value_weight)
        return logp[0], value_one[0]

    logp_all, value_all = lax.map(single, (boards, sides, legal_flat))
    return updated, logp_all.reshape(STEPS, POSITIONS, CELLS + 1), value_all.reshape(STEPS, POSITIONS)
```

```python
import functools

import jax
import jax.numpy as jnp
from jax import lax
from jax.experimental import pallas as pl
from jax.experimental.pallas import tpu as pltpu
from jax.sharding import PartitionSpec as P

BOARD = 19
CELLS = 361
PLANES = 4
PITCH = BOARD + 1
AXES = ("learn", "act")


def pairs(learners, actors, target):
    out = []
    for learner in range(learners):
        for actor in range(actors):
            to_learner, to_actor = target(learner, actor)
            out.append((learner * actors + actor, to_learner * actors + to_actor))
    return out


def route_mask(core, subset, bits):
    mask = 0
    for step in range(bits):
        if subset >> step & 1:
            mask |= 1 << (step if core == 0 else bits - 1 - step)
    return mask


def plane_route(learners, actors, step):
    low, high = 1 << step, learners >> (step + 1)
    return pairs(learners, actors, lambda l, a: (l ^ (low if a % 2 == 0 else high), a))


def reduce_gradients(gradients, learners, actors):
    bits = learners.bit_length() - 1
    me, core = lax.axis_index("learn"), lax.axis_index("act") % 2
    held = {}
    for subset in range(learners):
        layer = me ^ jnp.where(core == 0, route_mask(0, subset, bits), route_mask(1, subset, bits))
        held[subset] = lax.dynamic_index_in_dim(gradients, layer, 0, keepdims=False)
    for step in range(bits):
        route = plane_route(learners, actors, step)
        for subset in sorted(held, reverse=True):
            if subset >> step & 1:
                kept = subset ^ 1 << step
                held[kept] = held[kept] + lax.ppermute(held.pop(subset), AXES, route)
    return held[0]


def gather_blocks(own, learners, actors):
    bits = learners.bit_length() - 1
    chips = actors // 2

    def along_z(block, away):
        return lax.ppermute(block, AXES, pairs(learners, actors, lambda l, a: (l, a ^ (2 * away))))

    def along_plane(block, step):
        return lax.ppermute(block, AXES, plane_route(learners, actors, step))

    def swapped(block):
        return lax.ppermute(block, AXES, pairs(learners, actors, lambda l, a: (l, a ^ 1)))

    def label(away, subset):
        masks = (route_mask(0, subset, bits), route_mask(1, subset, bits))
        return masks, 2 * away

    def other_label(away, subset):
        masks, actor_mask = label(away, subset)
        return masks[::-1], actor_mask + 1

    found = []
    starts = {0: own}
    for away in range(1, chips):
        starts[away] = along_z(starts[away - 1], 1) if away % 2 and away > 1 else along_z(own, away)
    for away in range(chips):
        held = {0: starts[away]}
        for step in range(bits):
            for subset in sorted(held):
                held[subset | 1 << step] = along_plane(held[subset], step)
        groups = [sorted(held)] if away < chips - 1 else [sorted(held)[:-1], [learners - 1]]
        for group in groups:
            joined = jnp.concatenate([held[subset] for subset in group], axis=0) if len(group) > 1 else held[group[0]]
            found.append((swapped(joined), [other_label(away, subset) for subset in group]))
        found.extend((held[subset], [label(away, subset)]) for subset in sorted(held))
    return found


def place_of(masks, actor_mask):
    actor = lax.axis_index("act")
    mask = jnp.where(actor % 2 == 0, masks[0], masks[1])
    return lax.axis_index("learn") ^ mask, actor ^ actor_mask


def tower(places, layers, rows, number, width, cuts, *refs):
    blocks = refs[: len(places)]
    stem, legal, policy, passing, valuing, logp, extra = refs[len(places) : len(places) + 7]
    weights, field, stream, mask, arrived = refs[len(places) + 7 :]
    points = BOARD * width
    for labels, block in zip(places, blocks):
        if labels is None:
            for layer in range(layers):
                pltpu.make_async_copy(block.at[layer], weights.at[layer], arrived.at[layer]).start()
            continue
        for entry, label in enumerate(labels):
            layer, actor = place_of(*label)
            spot = pl.ds(pl.multiple_of(actor * rows, rows), rows)
            pltpu.make_async_copy(
                block.at[2 * entry : 2 * entry + 2], weights.at[layer, :, spot, :], arrived.at[layer]
            ).start()
    for half in range(2):
        field[half, :width, :] = jnp.zeros((width, field.shape[2]), jnp.bfloat16)
        field[half, width + points :, :] = jnp.zeros((width, field.shape[2]), jnp.bfloat16)
    column = lax.rem(lax.broadcasted_iota(jnp.int32, mask.shape, 0), width)
    on_board = (lax.rem(column, PITCH) < BOARD) & (column < PITCH * number)
    mask[...] = jnp.where(on_board, 1.0, 0.0)

    def rectified(low, high, values):
        keep = mask[low:high, :]
        keep = jnp.concatenate([keep] * (values.shape[1] // keep.shape[1]), axis=1)
        return jnp.maximum(values, 0.0) * keep

    def spread(half, low, high, values):
        values = rectified(low, high, values)
        depth = values.shape[1]
        spot = slice(width + low, width + high)
        field[half, spot, depth : 2 * depth] = values.astype(jnp.bfloat16)
        field[half, spot, :depth] = pltpu.roll(values, 1, 0).astype(jnp.bfloat16)
        field[half, spot, 2 * depth :] = pltpu.roll(values, high - low - 1, 0).astype(jnp.bfloat16)

    def convolve(half, layer, which, low, high):
        lines = [field[half, low + row * width : high + row * width, :] for row in range(3)]
        return jnp.dot(
            jnp.concatenate(lines, axis=1), weights[layer, which], preferred_element_type=jnp.float32
        )

    for low, high in cuts:
        values = stem[low:high, :]
        stream[low:high, :] = values
        spread(0, low, high, values)
    for layer in range(layers):
        pltpu.make_async_copy(weights.at[layer], weights.at[layer], arrived.at[layer]).wait()
        for low, high in cuts:
            spread(1, low, high, convolve(0, layer, 0, low, high))
        for low, high in cuts:
            values = stream[low:high, :] + convolve(1, layer, 1, low, high)
            if layer == layers - 1:
                stream[low:high, :] = rectified(low, high, values)
            else:
                stream[low:high, :] = values
                spread(0, low, high, values)

    trunk = stream[...]
    column = lax.rem(lax.broadcasted_iota(jnp.int32, (8, points), 1), width)
    owner = lax.broadcasted_iota(jnp.int32, (8, points), 0)
    inside = (column >= owner * PITCH) & (column < owner * PITCH + BOARD) & (owner < number)
    exact = functools.partial(
        lax.dot_general, precision=lax.Precision.HIGHEST, preferred_element_type=jnp.float32
    )
    per_point = jnp.broadcast_to(policy[...], (8, policy.shape[1]))
    raw = exact(per_point, trunk, (((1,), (1,)), ((), ())))
    pooled = exact(jnp.where(inside, 1.0, 0.0), trunk, (((1,), (0,)), ((), ()))) / CELLS
    pass_raw = jnp.sum(pooled * passing[...], axis=1, keepdims=True)
    value = jnp.tanh(jnp.sum(pooled * valuing[...], axis=1, keepdims=True))
    logits = 10.0 * jnp.tanh(raw / 10.0)
    pass_logit = 10.0 * jnp.tanh(pass_raw / 10.0)
    allowed = inside & (legal[...] > 0)
    shares = jnp.sum(jnp.where(allowed, jnp.exp(logits), 0.0), axis=1, keepdims=True)
    scale = jnp.log(shares + jnp.exp(pass_logit))
    logp[...] = jnp.where(allowed, logits - scale, 0.0)
    lane = lax.broadcasted_iota(jnp.int32, extra.shape, 1)
    extra[...] = jnp.where(lane == 0, pass_logit - scale, value)


def run_tower(found, layers, rows, depth, stem, legal, policy, passing, valuing, number, width):
    points = BOARD * width
    channels = stem.shape[1]
    places = [labels for _, labels in found]
    steps = [0, 7, 13, BOARD]
    cuts = [(low * width, high * width) for low, high in zip(steps, steps[1:])]
    anywhere = pl.BlockSpec(memory_space=pl.ANY)
    inside = pl.BlockSpec(memory_space=pltpu.VMEM)
    return pl.pallas_call(
        functools.partial(tower, places, layers, rows, number, width, cuts),
        out_shape=(
            jax.ShapeDtypeStruct((8, points), jnp.float32),
            jax.ShapeDtypeStruct((8, 128), jnp.float32),
        ),
        in_specs=[anywhere] * len(found) + [inside] * 5,
        out_specs=(inside, inside),
        scratch_shapes=[
            pltpu.VMEM((layers, 2, depth, channels), jnp.bfloat16),
            pltpu.VMEM((2, points + 2 * width, 3 * channels), jnp.bfloat16),
            pltpu.VMEM((points, channels), jnp.float32),
            pltpu.VMEM((points, 128), jnp.float32),
            pltpu.SemaphoreType.DMA((layers,)),
        ],
        compiler_params=pltpu.CompilerParams(vmem_limit_bytes=36 * 2**20),
        name="tower",
    )(*[block for block, _ in found], stem, legal, policy, passing, valuing)


def padded_boards(rows, width):
    number = rows.shape[0]
    boards = jnp.pad(rows.reshape(number, BOARD, BOARD), ((0, 0), (0, 0), (0, PITCH - BOARD)))
    side_by_side = jnp.swapaxes(boards, 0, 1).reshape(BOARD, number * PITCH)
    return jnp.pad(side_by_side, ((0, 0), (0, width - number * PITCH)))


def stem_stream(boards, sides, stem_weight, width):
    side_move = sides[:, None]
    planes = [boards == 1 + side_move, boards == 2 - side_move, boards == 0, jnp.ones_like(boards)]
    planes = [padded_boards(plane.astype(jnp.bfloat16), width) for plane in planes]
    field = jnp.stack(planes, axis=-1)[None]
    kernel = stem_weight.reshape(3, 3, PLANES, -1)
    out = lax.conv_general_dilated(
        field,
        kernel,
        (1, 1),
        ((1, 1), (1, 1)),
        dimension_numbers=("NHWC", "HWIO", "NHWC"),
        preferred_element_type=jnp.float32,
    )
    return out.reshape(BOARD * width, kernel.shape[-1])


def per_device(
    positions,
    to_move,
    legal_moves,
    master,
    gradients,
    stem_weight,
    policy_weight,
    pass_weight,
    value_weight,
):
    learners, actors = lax.axis_size("learn"), lax.axis_size("act")
    steps_here, local_count = positions.shape[:2]
    number = steps_here * local_count
    width = -(-number * PITCH // 8) * 8
    rows, channels = master.shape[2:]
    depth = rows * actors

    boards = positions.reshape(number, CELLS)
    stem = stem_stream(boards, to_move.reshape(number), stem_weight, width)
    legal = padded_boards(legal_moves.reshape(number, CELLS), width).reshape(1, BOARD * width)

    total = reduce_gradients(gradients[0], learners, actors)
    total, stem, legal = lax.optimization_barrier((total, stem, legal))
    updated = master[0] - total / learners
    found = gather_blocks(updated.astype(jnp.bfloat16), learners, actors)
    if rows % 16:
        whole = jnp.zeros((learners, 2, depth, channels), jnp.bfloat16)
        for block, labels in found:
            for entry, label in enumerate(labels):
                layer, actor = place_of(*label)
                piece = block[2 * entry : 2 * entry + 2]
                whole = lax.dynamic_update_slice(whole, piece[None], (layer, 0, actor * rows, 0))
        found = [(whole, None)]
    logp, extra = run_tower(
        found,
        learners,
        rows,
        depth,
        stem,
        legal,
        policy_weight[None],
        pass_weight[None],
        value_weight[None],
        number,
        width,
    )
    boards_out = logp[:number].reshape(number, BOARD, width)
    moves = [
        boards_out[board, :, board * PITCH : board * PITCH + BOARD].reshape(1, CELLS)
        for board in range(number)
    ]
    moves = jnp.concatenate([jnp.concatenate(moves, axis=0), extra[:number, :1]], axis=1)
    return (
        updated[None],
        moves.reshape(steps_here, local_count, CELLS + 1),
        extra[:number, 1].reshape(steps_here, local_count),
    )


def solution(mesh):
    in_specs = (
        P(None, ("learn", "act"), None),
        P(None, ("learn", "act")),
        P(None, ("learn", "act"), None),
        P("learn", None, "act", None),
        P("learn", None, None, "act", None),
        P(),
        P(),
        P(),
        P(),
    )
    out_specs = (
        P("learn", None, "act", None),
        P(None, ("learn", "act"), None),
        P(None, ("learn", "act")),
    )
    return jax.shard_map(
        per_device, mesh=mesh, in_specs=in_specs, out_specs=out_specs, check_vma=False
    )
```

```python
import functools

import jax
import jax.numpy as jnp
import numpy as np
from jax import lax
from jax.experimental import pallas as pl
from jax.experimental.pallas import tpu as pltpu
from jax.sharding import PartitionSpec as P

BOARD = 19
CELLS = 361
PLANES = 4
PITCH = BOARD + 1
AXES = ("learn", "act")


def pairs(learners, actors, target):
    out = []
    for learner in range(learners):
        for actor in range(actors):
            to_learner, to_actor = target(learner, actor)
            out.append((learner * actors + actor, to_learner * actors + to_actor))
    return out


def route_mask(core, subset, bits):
    mask = 0
    for step in range(bits):
        if subset >> step & 1:
            mask |= 1 << (step if core == 0 else bits - 1 - step)
    return mask


def plane_route(learners, actors, step):
    low, high = 1 << step, learners >> (step + 1)
    return pairs(learners, actors, lambda l, a: (l ^ (low if a % 2 == 0 else high), a))


def pick_kernel(subsets, bits, gradients, *refs):
    outs, arrived = refs[:-1], refs[-1]
    me, core = lax.axis_index("learn"), lax.axis_index("act") % 2
    copies = []
    for number, (subset, out) in enumerate(zip(subsets, outs)):
        layer = me ^ jnp.where(core == 0, route_mask(0, subset, bits), route_mask(1, subset, bits))
        copies.append(pltpu.make_async_copy(gradients.at[layer], out, arrived.at[number]))
        copies[-1].start()
    for copy in copies:
        copy.wait()


def pick(gradients, subsets, bits):
    shape = jax.ShapeDtypeStruct(gradients.shape[1:], gradients.dtype)
    return pl.pallas_call(
        functools.partial(pick_kernel, subsets, bits),
        out_shape=[shape] * len(subsets),
        in_specs=[pl.BlockSpec(memory_space=pl.ANY)],
        out_specs=[pl.BlockSpec(memory_space=pltpu.VMEM)] * len(subsets),
        scratch_shapes=[pltpu.SemaphoreType.DMA((len(subsets),))],
        compiler_params=pltpu.CompilerParams(vmem_limit_bytes=32 * 2**20),
        name="pick",
    )(gradients)


def reduce_gradients(gradients, learners, actors):
    bits = learners.bit_length() - 1
    order = sorted(range(learners), key=lambda subset: (not subset & 1, -subset))
    held, terms = {}, []
    for subsets in (order[:1], order[1:]):
        held.update(zip(subsets, pick(gradients, subsets, bits)))
    for step in range(bits):
        route = plane_route(learners, actors, step)
        for subset in sorted(held, reverse=True):
            if subset >> step & 1:
                kept = subset ^ 1 << step
                came = lax.ppermute(held.pop(subset), AXES, route)
                if kept:
                    held[kept] = held[kept] + came
                else:
                    terms.append(came)
    return held[0], *terms


def update_kernel(learners, *refs):
    *terms, master, updated, rounded = refs
    total = terms[0][...]
    for term in terms[1:]:
        total = total + term[...]
    new = master[...] - total / learners
    updated[...] = new
    rounded[...] = new.astype(jnp.bfloat16)


def update(terms, master, learners):
    inside = pl.BlockSpec(memory_space=pltpu.VMEM)
    return pl.pallas_call(
        functools.partial(update_kernel, learners),
        out_shape=(
            jax.ShapeDtypeStruct(master.shape, jnp.float32),
            jax.ShapeDtypeStruct(master.shape, jnp.bfloat16),
        ),
        in_specs=[inside] * (len(terms) + 1),
        out_specs=(inside, inside),
        compiler_params=pltpu.CompilerParams(vmem_limit_bytes=32 * 2**20),
        name="update",
    )(*terms, master)


def gather_blocks(own, learners, actors):
    bits = learners.bit_length() - 1
    chips = actors // 2

    def along_z(block, away):
        return lax.ppermute(block, AXES, pairs(learners, actors, lambda l, a: (l, a ^ (2 * away))))

    def along_plane(block, step):
        return lax.ppermute(block, AXES, plane_route(learners, actors, step))

    def swapped(block):
        return lax.ppermute(block, AXES, pairs(learners, actors, lambda l, a: (l, a ^ 1)))

    def label(away, subset):
        masks = (route_mask(0, subset, bits), route_mask(1, subset, bits))
        return masks, 2 * away

    def other_label(away, subset):
        masks, actor_mask = label(away, subset)
        return masks[::-1], actor_mask + 1

    found = []
    starts = {0: own}
    for away in range(1, chips):
        starts[away] = along_z(starts[away - 1], 1) if away % 2 and away > 1 else along_z(own, away)
    for away in range(chips):
        held = {0: starts[away]}
        for step in range(bits):
            for subset in sorted(held):
                if (away, subset | 1 << step) in ((1,3),):
                    held[subset | 1 << step] = along_z(before[subset | 1 << step], 1)
                else:
                    held[subset | 1 << step] = along_plane(held[subset], step)
        before = held
        groups = [sorted(held)] if away < chips - 1 else [sorted(held)[:-1], [learners - 1]]
        for group in groups:
            joined = jnp.concatenate([held[subset] for subset in group], axis=0) if len(group) > 1 else held[group[0]]
            found.append((swapped(joined), [other_label(away, subset) for subset in group]))
        found.extend((held[subset], [label(away, subset)]) for subset in sorted(held))
    return found


def place_of(masks, actor_mask):
    actor = lax.axis_index("act")
    mask = jnp.where(actor % 2 == 0, masks[0], masks[1])
    return lax.axis_index("learn") ^ mask, actor ^ actor_mask


def tower(places, layers, rows, number, width, cuts, *refs):
    blocks = refs[: len(places)]
    stem, legal, policy, passing, valuing, places_of_points, logp, worth = refs[len(places) : len(places) + 8]
    weights, field, stream, mask, arrived = refs[len(places) + 8 :]
    points = BOARD * width
    for labels, block in zip(places, blocks):
        if labels is None:
            for layer in range(layers):
                pltpu.make_async_copy(block.at[layer], weights.at[layer], arrived.at[layer]).start()
            continue
        for entry, label in enumerate(labels):
            layer, actor = place_of(*label)
            spot = pl.ds(pl.multiple_of(actor * rows, rows), rows)
            pltpu.make_async_copy(
                block.at[2 * entry : 2 * entry + 2], weights.at[layer, :, spot, :], arrived.at[layer]
            ).start()
    for half in range(2):
        field[half, :width, :] = jnp.zeros((width, field.shape[2]), jnp.bfloat16)
        field[half, width + points :, :] = jnp.zeros((width, field.shape[2]), jnp.bfloat16)
    column = lax.rem(lax.broadcasted_iota(jnp.int32, mask.shape, 0), width)
    on_board = (lax.rem(column, PITCH) < BOARD) & (column < PITCH * number)
    mask[...] = jnp.where(on_board, 1.0, 0.0)

    def rectified(low, high, values):
        keep = mask[low:high, :]
        keep = jnp.concatenate([keep] * (values.shape[1] // keep.shape[1]), axis=1)
        return jnp.maximum(values, 0.0) * keep

    def spread(half, low, high, values):
        values = rectified(low, high, values)
        depth = values.shape[1]
        spot = slice(width + low, width + high)
        field[half, spot, depth : 2 * depth] = values.astype(jnp.bfloat16)
        field[half, spot, :depth] = pltpu.roll(values, 1, 0).astype(jnp.bfloat16)
        field[half, spot, 2 * depth :] = pltpu.roll(values, high - low - 1, 0).astype(jnp.bfloat16)

    def convolve(half, layer, which, low, high):
        lines = [field[half, low + row * width : high + row * width, :] for row in range(3)]
        return jnp.dot(
            jnp.concatenate(lines, axis=1), weights[layer, which], preferred_element_type=jnp.float32
        )

    for low, high in cuts:
        values = stem[low:high, :]
        stream[low:high, :] = values
        spread(0, low, high, values)
    for layer in range(layers):
        pltpu.make_async_copy(weights.at[layer], weights.at[layer], arrived.at[layer]).wait()
        for low, high in cuts:
            spread(1, low, high, convolve(0, layer, 0, low, high))
        for low, high in cuts:
            values = stream[low:high, :] + convolve(1, layer, 1, low, high)
            if layer == layers - 1:
                stream[low:high, :] = rectified(low, high, values)
            else:
                stream[low:high, :] = values
                spread(0, low, high, values)

    trunk = stream[...]
    column = lax.rem(lax.broadcasted_iota(jnp.int32, (8, points), 1), width)
    owner = lax.broadcasted_iota(jnp.int32, (8, points), 0)
    inside = (column >= owner * PITCH) & (column < owner * PITCH + BOARD) & (owner < number)
    exact = functools.partial(
        lax.dot_general, precision=lax.Precision.HIGHEST, preferred_element_type=jnp.float32
    )
    per_point = jnp.broadcast_to(policy[...], (8, policy.shape[1]))
    raw = exact(per_point, trunk, (((1,), (1,)), ((), ())))
    pooled = exact(jnp.where(inside, 1.0, 0.0), trunk, (((1,), (0,)), ((), ()))) / CELLS
    pass_raw = jnp.sum(pooled * passing[...], axis=1, keepdims=True)
    value = jnp.tanh(jnp.sum(pooled * valuing[...], axis=1, keepdims=True))
    logits = 10.0 * jnp.tanh(raw / 10.0)
    pass_logit = 10.0 * jnp.tanh(pass_raw / 10.0)
    allowed = inside & (legal[...] > 0)
    shares = jnp.sum(jnp.where(allowed, jnp.exp(logits), 0.0), axis=1, keepdims=True)
    scale = jnp.log(shares + jnp.exp(pass_logit))
    padded = jnp.where(allowed, logits - scale, 0.0)
    parts, rest = [], padded
    for _ in range(3):
        parts.append(rest.astype(jnp.bfloat16))
        rest = rest - parts[-1].astype(jnp.float32)
    parts = jnp.concatenate(parts, axis=0)
    moved = jnp.dot(parts, places_of_points[...], preferred_element_type=jnp.float32)
    packed = moved[:8] + moved[8:16] + moved[16:]
    lane = lax.broadcasted_iota(jnp.int32, packed.shape, 1)
    packed = jnp.where(lane == CELLS, pass_logit - scale, packed)
    steps_here, local_count = logp.shape[:2]
    for board in range(number):
        step, local = divmod(board, local_count)
        logp[step, local : local + 1, :] = packed[board : board + 1, : CELLS + 1]
        worth[local : local + 1, step : step + 1] = value[board : board + 1, :]


def run_tower(found, layers, rows, depth, stem, legal, policy, passing, valuing, steps_here, local_count, width):
    number = steps_here * local_count
    point = np.arange(BOARD * width)
    column = point % width
    cell = point // width * BOARD + column % PITCH
    known = (column % PITCH < BOARD) & (column < PITCH * number)
    lanes = -(-(CELLS + 1) // 128) * 128
    target = np.where(known, cell, lanes)[:, None] == np.arange(lanes)[None]
    places_of_points = jnp.asarray(target.astype(jnp.bfloat16))
    points = BOARD * width
    channels = stem.shape[1]
    places = [labels for _, labels in found]
    steps = [0, 7, 13, BOARD]
    cuts = [(low * width, high * width) for low, high in zip(steps, steps[1:])]
    anywhere = pl.BlockSpec(memory_space=pl.ANY)
    inside = pl.BlockSpec(memory_space=pltpu.VMEM)
    return pl.pallas_call(
        functools.partial(tower, places, layers, rows, number, width, cuts),
        out_shape=(
            jax.ShapeDtypeStruct((steps_here, local_count, CELLS + 1), jnp.float32),
            jax.ShapeDtypeStruct((local_count, steps_here), jnp.float32),
        ),
        in_specs=[anywhere] * len(found) + [inside] * 6,
        out_specs=(inside, inside),
        scratch_shapes=[
            pltpu.VMEM((layers, 2, depth, channels), jnp.bfloat16),
            pltpu.VMEM((2, points + 2 * width, 3 * channels), jnp.bfloat16),
            pltpu.VMEM((points, channels), jnp.float32),
            pltpu.VMEM((points, 128), jnp.float32),
            pltpu.SemaphoreType.DMA((layers,)),
        ],
        compiler_params=pltpu.CompilerParams(vmem_limit_bytes=36 * 2**20),
        name="tower",
    )(*[block for block, _ in found], stem, legal, policy, passing, valuing, places_of_points)


def padded_boards(rows, width):
    number = rows.shape[0]
    boards = jnp.pad(rows.reshape(number, BOARD, BOARD), ((0, 0), (0, 0), (0, PITCH - BOARD)))
    side_by_side = jnp.swapaxes(boards, 0, 1).reshape(BOARD, number * PITCH)
    return jnp.pad(side_by_side, ((0, 0), (0, width - number * PITCH)))


def stem_stream(boards, sides, stem_weight, width):
    side_move = sides[:, None]
    planes = [boards == 1 + side_move, boards == 2 - side_move, boards == 0, jnp.ones_like(boards)]
    planes = [padded_boards(plane.astype(jnp.bfloat16), width) for plane in planes]
    field = jnp.stack(planes, axis=-1)[None]
    kernel = stem_weight.reshape(3, 3, PLANES, -1)
    out = lax.conv_general_dilated(
        field,
        kernel,
        (1, 1),
        ((1, 1), (1, 1)),
        dimension_numbers=("NHWC", "HWIO", "NHWC"),
        preferred_element_type=jnp.float32,
    )
    return out.reshape(BOARD * width, kernel.shape[-1])


def per_device(
    positions,
    to_move,
    legal_moves,
    master,
    gradients,
    stem_weight,
    policy_weight,
    pass_weight,
    value_weight,
):
    learners, actors = lax.axis_size("learn"), lax.axis_size("act")
    steps_here, local_count = positions.shape[:2]
    number = steps_here * local_count
    width = -(-number * PITCH // 8) * 8
    rows, channels = master.shape[2:]
    depth = rows * actors

    boards = positions.reshape(number, CELLS)
    stem = stem_stream(boards, to_move.reshape(number), stem_weight, width)
    legal = padded_boards(legal_moves.reshape(number, CELLS), width).reshape(1, BOARD * width)

    terms = reduce_gradients(gradients[0], learners, actors)
    *terms, stem, legal = lax.optimization_barrier((*terms, stem, legal))
    updated, rounded = update(terms, master[0], learners)
    found = gather_blocks(rounded, learners, actors)
    if rows % 16:
        whole = jnp.zeros((learners, 2, depth, channels), jnp.bfloat16)
        for block, labels in found:
            for entry, label in enumerate(labels):
                layer, actor = place_of(*label)
                piece = block[2 * entry : 2 * entry + 2]
                whole = lax.dynamic_update_slice(whole, piece[None], (layer, 0, actor * rows, 0))
        found = [(whole, None)]
    logp, values = run_tower(
        found,
        learners,
        rows,
        depth,
        stem,
        legal,
        policy_weight[None],
        pass_weight[None],
        value_weight[None],
        steps_here,
        local_count,
        width,
    )
    return updated[None], logp, values.T


def solution(mesh):
    in_specs = (
        P(None, ("learn", "act"), None),
        P(None, ("learn", "act")),
        P(None, ("learn", "act"), None),
        P("learn", None, "act", None),
        P("learn", None, None, "act", None),
        P(),
        P(),
        P(),
        P(),
    )
    out_specs = (
        P("learn", None, "act", None),
        P(None, ("learn", "act"), None),
        P(None, ("learn", "act")),
    )
    return jax.shard_map(
        per_device, mesh=mesh, in_specs=in_specs, out_specs=out_specs, check_vma=False
    )
```

```python
import functools

import jax
import jax.numpy as jnp
import numpy as np
from jax import lax
from jax.experimental import pallas as pl
from jax.experimental.pallas import tpu as pltpu
from jax.sharding import PartitionSpec as P

BOARD = 19
CELLS = 361
PLANES = 4
PITCH = BOARD + 1
AXES = ("learn", "act")


def pairs(learners, actors, target):
    out = []
    for learner in range(learners):
        for actor in range(actors):
            to_learner, to_actor = target(learner, actor)
            out.append((learner * actors + actor, to_learner * actors + to_actor))
    return out


def route_mask(core, subset, bits):
    mask = 0
    for step in range(bits):
        if subset >> step & 1:
            mask |= 1 << (step if core == 0 else bits - 1 - step)
    return mask


def plane_route(learners, actors, step):
    low, high = 1 << step, learners >> (step + 1)
    return pairs(learners, actors, lambda l, a: (l ^ (low if a % 2 == 0 else high), a))


def pick_kernel(subsets, bits, gradients, *refs):
    outs, arrived = refs[:-1], refs[-1]
    me, core = lax.axis_index("learn"), lax.axis_index("act") % 2
    copies = []
    for number, (subset, out) in enumerate(zip(subsets, outs)):
        layer = me ^ jnp.where(core == 0, route_mask(0, subset, bits), route_mask(1, subset, bits))
        copies.append(pltpu.make_async_copy(gradients.at[layer], out, arrived.at[number]))
        copies[-1].start()
    for copy in copies:
        copy.wait()


def pick(gradients, subsets, bits):
    shape = jax.ShapeDtypeStruct(gradients.shape[1:], gradients.dtype)
    return pl.pallas_call(
        functools.partial(pick_kernel, subsets, bits),
        out_shape=[shape] * len(subsets),
        in_specs=[pl.BlockSpec(memory_space=pl.ANY)],
        out_specs=[pl.BlockSpec(memory_space=pltpu.VMEM)] * len(subsets),
        scratch_shapes=[pltpu.SemaphoreType.DMA((len(subsets),))],
        compiler_params=pltpu.CompilerParams(vmem_limit_bytes=32 * 2**20),
        name="pick",
    )(gradients)


def reduce_gradients(gradients, learners, actors):
    bits = learners.bit_length() - 1
    order = sorted(range(learners), key=lambda subset: (not subset & 1, -subset))
    held, terms = {}, []
    me, core = lax.axis_index("learn"), lax.axis_index("act") % 2
    layer = me ^ jnp.where(core == 0, route_mask(0, order[0], bits), route_mask(1, order[0], bits))
    held[order[0]] = lax.dynamic_index_in_dim(gradients, layer, 0, keepdims=False)
    held.update(zip(order[1:], pick(gradients, order[1:], bits)))
    for step in range(bits):
        route = plane_route(learners, actors, step)
        for subset in sorted(held, reverse=True):
            if subset >> step & 1:
                kept = subset ^ 1 << step
                came = lax.ppermute(held.pop(subset), AXES, route)
                if kept:
                    held[kept] = held[kept] + came
                else:
                    terms.append(came)
    return held[0], *terms


def update_kernel(learners, *refs):
    *terms, master, updated, rounded = refs
    total = terms[0][...]
    for term in terms[1:]:
        total = total + term[...]
    new = master[...] - total / learners
    updated[...] = new
    rounded[...] = new.astype(jnp.bfloat16)


def update(terms, master, learners):
    inside = pl.BlockSpec(memory_space=pltpu.VMEM)
    return pl.pallas_call(
        functools.partial(update_kernel, learners),
        out_shape=(
            jax.ShapeDtypeStruct(master.shape, jnp.float32),
            jax.ShapeDtypeStruct(master.shape, jnp.bfloat16),
        ),
        in_specs=[inside] * (len(terms) + 1),
        out_specs=(inside, inside),
        compiler_params=pltpu.CompilerParams(vmem_limit_bytes=32 * 2**20),
        name="update",
    )(*terms, master)


def gather_blocks(own, learners, actors):
    bits = learners.bit_length() - 1
    chips = actors // 2

    def along_z(block, away):
        return lax.ppermute(block, AXES, pairs(learners, actors, lambda l, a: (l, a ^ (2 * away))))

    def along_plane(block, step):
        return lax.ppermute(block, AXES, plane_route(learners, actors, step))

    def swapped(block):
        return lax.ppermute(block, AXES, pairs(learners, actors, lambda l, a: (l, a ^ 1)))

    def label(away, subset):
        masks = (route_mask(0, subset, bits), route_mask(1, subset, bits))
        return masks, 2 * away

    def other_label(away, subset):
        masks, actor_mask = label(away, subset)
        return masks[::-1], actor_mask + 1

    found = []
    starts = {0: own}
    for away in range(1, chips):
        starts[away] = along_z(starts[away - 1], 1) if away % 2 and away > 1 else along_z(own, away)
    for away in range(chips):
        held = {0: starts[away]}
        for step in range(bits):
            for subset in sorted(held):
                if (away, subset | 1 << step) in ((1,3),):
                    held[subset | 1 << step] = along_z(before[subset | 1 << step], 1)
                else:
                    held[subset | 1 << step] = along_plane(held[subset], step)
        before = held
        groups = [sorted(held)] if away < chips - 1 else [sorted(held)[:-1], [learners - 1]]
        for group in groups:
            joined = jnp.concatenate([held[subset] for subset in group], axis=0) if len(group) > 1 else held[group[0]]
            found.append((swapped(joined), [other_label(away, subset) for subset in group]))
        found.extend((held[subset], [label(away, subset)]) for subset in sorted(held))
    return found


def place_of(masks, actor_mask):
    actor = lax.axis_index("act")
    mask = jnp.where(actor % 2 == 0, masks[0], masks[1])
    return lax.axis_index("learn") ^ mask, actor ^ actor_mask


def tower(places, layers, rows, number, width, cuts, *refs):
    blocks = refs[: len(places)]
    stem, legal, policy, passing, valuing, places_of_points, logp, worth = refs[len(places) : len(places) + 8]
    weights, field, stream, mask, arrived = refs[len(places) + 8 :]
    points = BOARD * width
    for labels, block in zip(places, blocks):
        if labels is None:
            for layer in range(layers):
                pltpu.make_async_copy(block.at[layer], weights.at[layer], arrived.at[layer]).start()
            continue
        for entry, label in enumerate(labels):
            layer, actor = place_of(*label)
            spot = pl.ds(pl.multiple_of(actor * rows, rows), rows)
            pltpu.make_async_copy(
                block.at[2 * entry : 2 * entry + 2], weights.at[layer, :, spot, :], arrived.at[layer]
            ).start()
    for half in range(2):
        field[half, :width, :] = jnp.zeros((width, field.shape[2]), jnp.bfloat16)
        field[half, width + points :, :] = jnp.zeros((width, field.shape[2]), jnp.bfloat16)
    column = lax.rem(lax.broadcasted_iota(jnp.int32, mask.shape, 0), width)
    on_board = (lax.rem(column, PITCH) < BOARD) & (column < PITCH * number)
    mask[...] = jnp.where(on_board, 1.0, 0.0)

    def rectified(low, high, values):
        keep = mask[low:high, :]
        keep = jnp.concatenate([keep] * (values.shape[1] // keep.shape[1]), axis=1)
        return jnp.maximum(values, 0.0) * keep

    def spread(half, low, high, values):
        values = rectified(low, high, values)
        depth = values.shape[1]
        spot = slice(width + low, width + high)
        field[half, spot, depth : 2 * depth] = values.astype(jnp.bfloat16)
        field[half, spot, :depth] = pltpu.roll(values, 1, 0).astype(jnp.bfloat16)
        field[half, spot, 2 * depth :] = pltpu.roll(values, high - low - 1, 0).astype(jnp.bfloat16)

    def convolve(half, layer, which, low, high):
        lines = [field[half, low + row * width : high + row * width, :] for row in range(3)]
        return jnp.dot(
            jnp.concatenate(lines, axis=1), weights[layer, which], preferred_element_type=jnp.float32
        )

    for low, high in cuts:
        values = stem[low:high, :]
        stream[low:high, :] = values
        spread(0, low, high, values)
    for layer in range(layers):
        pltpu.make_async_copy(weights.at[layer], weights.at[layer], arrived.at[layer]).wait()
        for low, high in cuts:
            spread(1, low, high, convolve(0, layer, 0, low, high))
        for low, high in cuts:
            values = stream[low:high, :] + convolve(1, layer, 1, low, high)
            if layer == layers - 1:
                stream[low:high, :] = rectified(low, high, values)
            else:
                stream[low:high, :] = values
                spread(0, low, high, values)

    trunk = stream[...]
    column = lax.rem(lax.broadcasted_iota(jnp.int32, (8, points), 1), width)
    owner = lax.broadcasted_iota(jnp.int32, (8, points), 0)
    inside = (column >= owner * PITCH) & (column < owner * PITCH + BOARD) & (owner < number)
    exact = functools.partial(
        lax.dot_general, precision=lax.Precision.HIGHEST, preferred_element_type=jnp.float32
    )
    per_point = jnp.broadcast_to(policy[...], (8, policy.shape[1]))
    raw = exact(per_point, trunk, (((1,), (1,)), ((), ())))
    pooled = exact(jnp.where(inside, 1.0, 0.0), trunk, (((1,), (0,)), ((), ()))) / CELLS
    pass_raw = jnp.sum(pooled * passing[...], axis=1, keepdims=True)
    value = jnp.tanh(jnp.sum(pooled * valuing[...], axis=1, keepdims=True))
    logits = 10.0 * jnp.tanh(raw / 10.0)
    pass_logit = 10.0 * jnp.tanh(pass_raw / 10.0)
    allowed = inside & (legal[...] > 0)
    shares = jnp.sum(jnp.where(allowed, jnp.exp(logits), 0.0), axis=1, keepdims=True)
    scale = jnp.log(shares + jnp.exp(pass_logit))
    padded = jnp.where(allowed, logits - scale, 0.0)
    parts, rest = [], padded
    for _ in range(3):
        parts.append(rest.astype(jnp.bfloat16))
        rest = rest - parts[-1].astype(jnp.float32)
    parts = jnp.concatenate(parts, axis=0)
    moved = jnp.dot(parts, places_of_points[...], preferred_element_type=jnp.float32)
    packed = moved[:8] + moved[8:16] + moved[16:]
    lane = lax.broadcasted_iota(jnp.int32, packed.shape, 1)
    packed = jnp.where(lane == CELLS, pass_logit - scale, packed)
    steps_here, local_count = logp.shape[:2]
    for board in range(number):
        step, local = divmod(board, local_count)
        logp[step, local : local + 1, :] = packed[board : board + 1, : CELLS + 1]
        worth[local : local + 1, step : step + 1] = value[board : board + 1, :]


def run_tower(found, layers, rows, depth, stem, legal, policy, passing, valuing, steps_here, local_count, width):
    number = steps_here * local_count
    point = np.arange(BOARD * width)
    column = point % width
    cell = point // width * BOARD + column % PITCH
    known = (column % PITCH < BOARD) & (column < PITCH * number)
    lanes = -(-(CELLS + 1) // 128) * 128
    target = np.where(known, cell, lanes)[:, None] == np.arange(lanes)[None]
    places_of_points = jnp.asarray(target.astype(jnp.bfloat16))
    points = BOARD * width
    channels = stem.shape[1]
    places = [labels for _, labels in found]
    steps = [0, 5, 10, 15, BOARD]
    cuts = [(low * width, high * width) for low, high in zip(steps, steps[1:])]
    anywhere = pl.BlockSpec(memory_space=pl.ANY)
    inside = pl.BlockSpec(memory_space=pltpu.VMEM)
    return pl.pallas_call(
        functools.partial(tower, places, layers, rows, number, width, cuts),
        out_shape=(
            jax.ShapeDtypeStruct((steps_here, local_count, CELLS + 1), jnp.float32),
            jax.ShapeDtypeStruct((local_count, steps_here), jnp.float32),
        ),
        in_specs=[anywhere] * len(found) + [inside] * 6,
        out_specs=(inside, inside),
        scratch_shapes=[
            pltpu.VMEM((layers, 2, depth, channels), jnp.bfloat16),
            pltpu.VMEM((2, points + 2 * width, 3 * channels), jnp.bfloat16),
            pltpu.VMEM((points, channels), jnp.float32),
            pltpu.VMEM((points, 128), jnp.float32),
            pltpu.SemaphoreType.DMA((layers,)),
        ],
        compiler_params=pltpu.CompilerParams(vmem_limit_bytes=36 * 2**20),
        name="tower",
    )(*[block for block, _ in found], stem, legal, policy, passing, valuing, places_of_points)


def padded_boards(rows, width):
    number = rows.shape[0]
    boards = jnp.pad(rows.reshape(number, BOARD, BOARD), ((0, 0), (0, 0), (0, PITCH - BOARD)))
    side_by_side = jnp.swapaxes(boards, 0, 1).reshape(BOARD, number * PITCH)
    return jnp.pad(side_by_side, ((0, 0), (0, width - number * PITCH)))


def stem_stream(boards, sides, stem_weight, width):
    side_move = sides[:, None]
    planes = [boards == 1 + side_move, boards == 2 - side_move, boards == 0, jnp.ones_like(boards)]
    planes = [padded_boards(plane.astype(jnp.bfloat16), width) for plane in planes]
    field = jnp.stack(planes, axis=-1)[None]
    kernel = stem_weight.reshape(3, 3, PLANES, -1)
    out = lax.conv_general_dilated(
        field,
        kernel,
        (1, 1),
        ((1, 1), (1, 1)),
        dimension_numbers=("NHWC", "HWIO", "NHWC"),
        preferred_element_type=jnp.float32,
    )
    return out.reshape(BOARD * width, kernel.shape[-1])


def per_device(
    positions,
    to_move,
    legal_moves,
    master,
    gradients,
    stem_weight,
    policy_weight,
    pass_weight,
    value_weight,
):
    learners, actors = lax.axis_size("learn"), lax.axis_size("act")
    steps_here, local_count = positions.shape[:2]
    number = steps_here * local_count
    width = -(-number * PITCH // 8) * 8
    rows, channels = master.shape[2:]
    depth = rows * actors

    boards = positions.reshape(number, CELLS)
    stem = stem_stream(boards, to_move.reshape(number), stem_weight, width)
    legal = padded_boards(legal_moves.reshape(number, CELLS), width).reshape(1, BOARD * width)

    terms = reduce_gradients(gradients[0], learners, actors)
    *terms, stem, legal = lax.optimization_barrier((*terms, stem, legal))
    updated, rounded = update(terms, master[0], learners)
    found = gather_blocks(rounded, learners, actors)
    if rows % 16:
        whole = jnp.zeros((learners, 2, depth, channels), jnp.bfloat16)
        for block, labels in found:
            for entry, label in enumerate(labels):
                layer, actor = place_of(*label)
                piece = block[2 * entry : 2 * entry + 2]
                whole = lax.dynamic_update_slice(whole, piece[None], (layer, 0, actor * rows, 0))
        found = [(whole, None)]
    logp, values = run_tower(
        found,
        learners,
        rows,
        depth,
        stem,
        legal,
        policy_weight[None],
        pass_weight[None],
        value_weight[None],
        steps_here,
        local_count,
        width,
    )
    return updated[None], logp, values.T


def solution(mesh):
    in_specs = (
        P(None, ("learn", "act"), None),
        P(None, ("learn", "act")),
        P(None, ("learn", "act"), None),
        P("learn", None, "act", None),
        P("learn", None, None, "act", None),
        P(),
        P(),
        P(),
        P(),
    )
    out_specs = (
        P("learn", None, "act", None),
        P(None, ("learn", "act"), None),
        P(None, ("learn", "act")),
    )
    return jax.shard_map(
        per_device, mesh=mesh, in_specs=in_specs, out_specs=out_specs, check_vma=False
    )
```

```python
import functools

import jax
import jax.numpy as jnp
import numpy as np
from jax import lax
from jax.experimental import pallas as pl
from jax.experimental.pallas import tpu as pltpu
from jax.sharding import PartitionSpec as P

BOARD = 19
CELLS = 361
PLANES = 4
PITCH = BOARD + 1
AXES = ("learn", "act")


def pairs(learners, actors, target):
    out = []
    for learner in range(learners):
        for actor in range(actors):
            to_learner, to_actor = target(learner, actor)
            out.append((learner * actors + actor, to_learner * actors + to_actor))
    return out


def route_mask(core, subset, bits):
    mask = 0
    for step in range(bits):
        if subset >> step & 1:
            mask |= 1 << (step if core == 0 else bits - 1 - step)
    return mask


def plane_route(learners, actors, step):
    low, high = 1 << step, learners >> (step + 1)
    return pairs(learners, actors, lambda l, a: (l ^ (low if a % 2 == 0 else high), a))


def pick_kernel(subsets, bits, gradients, *refs):
    outs, arrived = refs[:-1], refs[-1]
    me, core = lax.axis_index("learn"), lax.axis_index("act") % 2
    copies = []
    for number, (subset, out) in enumerate(zip(subsets, outs)):
        layer = me ^ jnp.where(core == 0, route_mask(0, subset, bits), route_mask(1, subset, bits))
        copies.append(pltpu.make_async_copy(gradients.at[layer], out, arrived.at[number]))
        copies[-1].start()
    for copy in copies:
        copy.wait()


def pick(gradients, subsets, bits):
    shape = jax.ShapeDtypeStruct(gradients.shape[1:], gradients.dtype)
    return pl.pallas_call(
        functools.partial(pick_kernel, subsets, bits),
        out_shape=[shape] * len(subsets),
        in_specs=[pl.BlockSpec(memory_space=pl.ANY)],
        out_specs=[pl.BlockSpec(memory_space=pltpu.VMEM)] * len(subsets),
        scratch_shapes=[pltpu.SemaphoreType.DMA((len(subsets),))],
        compiler_params=pltpu.CompilerParams(vmem_limit_bytes=32 * 2**20),
        name="pick",
    )(gradients)


def reduce_gradients(gradients, learners, actors):
    bits = learners.bit_length() - 1
    order = sorted(range(learners), key=lambda subset: (not subset & 1, -subset))
    held, terms = {}, []
    me, core = lax.axis_index("learn"), lax.axis_index("act") % 2
    layer = me ^ jnp.where(core == 0, route_mask(0, order[0], bits), route_mask(1, order[0], bits))
    held[order[0]] = lax.dynamic_index_in_dim(gradients, layer, 0, keepdims=False)
    held.update(zip(order[1:], pick(gradients, order[1:], bits)))
    for step in range(bits):
        route = plane_route(learners, actors, step)
        for subset in sorted(held, reverse=True):
            if subset >> step & 1:
                kept = subset ^ 1 << step
                came = lax.ppermute(held.pop(subset), AXES, route)
                if kept:
                    held[kept] = held[kept] + came
                else:
                    terms.append(came)
    return held[0], *terms


def update_kernel(learners, *refs):
    *terms, master, updated, rounded = refs
    total = terms[0][...]
    for term in terms[1:]:
        total = total + term[...]
    new = master[...] - total / learners
    updated[...] = new
    rounded[...] = new.astype(jnp.bfloat16)


def update(terms, master, learners):
    inside = pl.BlockSpec(memory_space=pltpu.VMEM)
    return pl.pallas_call(
        functools.partial(update_kernel, learners),
        out_shape=(
            jax.ShapeDtypeStruct(master.shape, jnp.float32),
            jax.ShapeDtypeStruct(master.shape, jnp.bfloat16),
        ),
        in_specs=[inside] * (len(terms) + 1),
        out_specs=(inside, inside),
        compiler_params=pltpu.CompilerParams(vmem_limit_bytes=32 * 2**20),
        name="update",
    )(*terms, master)


def gather_blocks(own, learners, actors):
    bits = learners.bit_length() - 1
    chips = actors // 2

    def along_z(block, away):
        return lax.ppermute(block, AXES, pairs(learners, actors, lambda l, a: (l, a ^ (2 * away))))

    def along_plane(block, step):
        return lax.ppermute(block, AXES, plane_route(learners, actors, step))

    def swapped(block):
        return lax.ppermute(block, AXES, pairs(learners, actors, lambda l, a: (l, a ^ 1)))

    def label(away, subset):
        masks = (route_mask(0, subset, bits), route_mask(1, subset, bits))
        return masks, 2 * away

    def other_label(away, subset):
        masks, actor_mask = label(away, subset)
        return masks[::-1], actor_mask + 1

    found = []
    starts = {0: own}
    for away in range(1, chips):
        starts[away] = along_z(starts[away - 1], 1) if away % 2 and away > 1 else along_z(own, away)
    for away in range(chips):
        held = {0: starts[away]}
        for step in range(bits):
            for subset in sorted(held):
                if (away, subset | 1 << step) in ((1,3),):
                    held[subset | 1 << step] = along_z(before[subset | 1 << step], 1)
                else:
                    held[subset | 1 << step] = along_plane(held[subset], step)
        before = held
        groups = [sorted(held)] if away < chips - 1 else [sorted(held)[:-1], [learners - 1]]
        for group in groups:
            joined = jnp.concatenate([held[subset] for subset in group], axis=0) if len(group) > 1 else held[group[0]]
            found.append((swapped(joined), [other_label(away, subset) for subset in group]))
        found.extend((held[subset], [label(away, subset)]) for subset in sorted(held))
    return found


def place_of(masks, actor_mask):
    actor = lax.axis_index("act")
    mask = jnp.where(actor % 2 == 0, masks[0], masks[1])
    return lax.axis_index("learn") ^ mask, actor ^ actor_mask


def tower(places, layers, rows, number, width, cuts, *refs):
    blocks = refs[: len(places)]
    stem, legal, policy, passing, valuing, places_of_points, logp, worth = refs[len(places) : len(places) + 8]
    weights, field, stream, mask, of_board, arrived = refs[len(places) + 8 :]
    points = BOARD * width
    for labels, block in zip(places, blocks):
        if labels is None:
            for layer in range(layers):
                pltpu.make_async_copy(block.at[layer], weights.at[layer], arrived.at[layer]).start()
            continue
        for entry, label in enumerate(labels):
            layer, actor = place_of(*label)
            spot = pl.ds(pl.multiple_of(actor * rows, rows), rows)
            pltpu.make_async_copy(
                block.at[2 * entry : 2 * entry + 2], weights.at[layer, :, spot, :], arrived.at[layer]
            ).start()
    for half in range(2):
        field[half, :width, :] = jnp.zeros((width, field.shape[2]), jnp.bfloat16)
        field[half, width + points :, :] = jnp.zeros((width, field.shape[2]), jnp.bfloat16)
    column = lax.rem(lax.broadcasted_iota(jnp.int32, mask.shape, 0), width)
    on_board = (lax.rem(column, PITCH) < BOARD) & (column < PITCH * number)
    mask[...] = jnp.where(on_board, 1.0, 0.0)
    for board in range(number):
        of_board[board] = jnp.where((column >= board * PITCH) & (column < (board + 1) * PITCH), 1.0, 0.0)

    def rectified(low, high, values):
        keep = mask[low:high, :]
        keep = jnp.concatenate([keep] * (values.shape[1] // keep.shape[1]), axis=1)
        return jnp.maximum(values, 0.0) * keep

    def spread(half, low, high, values):
        values = rectified(low, high, values)
        depth = values.shape[1]
        spot = slice(width + low, width + high)
        field[half, spot, depth : 2 * depth] = values.astype(jnp.bfloat16)
        field[half, spot, :depth] = pltpu.roll(values, 1, 0).astype(jnp.bfloat16)
        field[half, spot, 2 * depth :] = pltpu.roll(values, high - low - 1, 0).astype(jnp.bfloat16)

    def convolve(half, layer, which, low, high):
        lines = [field[half, low + row * width : high + row * width, :] for row in range(3)]
        return jnp.dot(
            jnp.concatenate(lines, axis=1), weights[layer, which], preferred_element_type=jnp.float32
        )

    for low, high in cuts:
        values = stem[low:high, :]
        stream[low:high, :] = values
        spread(0, low, high, values)
    for layer in range(layers):
        pltpu.make_async_copy(weights.at[layer], weights.at[layer], arrived.at[layer]).wait()
        for low, high in cuts:
            spread(1, low, high, convolve(0, layer, 0, low, high))
        for low, high in cuts:
            values = stream[low:high, :] + convolve(1, layer, 1, low, high)
            if layer == layers - 1:
                stream[low:high, :] = rectified(low, high, values)
            else:
                stream[low:high, :] = values
                spread(0, low, high, values)

    trunk = stream[...]
    column = lax.rem(lax.broadcasted_iota(jnp.int32, (8, points), 1), width)
    owner = lax.broadcasted_iota(jnp.int32, (8, points), 0)
    inside = (column >= owner * PITCH) & (column < owner * PITCH + BOARD) & (owner < number)
    exact = functools.partial(
        lax.dot_general, precision=lax.Precision.HIGHEST, preferred_element_type=jnp.float32
    )
    weighted = trunk * policy[...]
    weighted = sum(weighted[:, part : part + 128] for part in range(0, weighted.shape[1], 128))
    raw = exact(jnp.ones((8, 128), jnp.float32), weighted, (((1,), (1,)), ((), ())))
    sums = [
        jnp.sum(trunk * jnp.concatenate([of_board[board]] * (trunk.shape[1] // 128), axis=1), axis=0, keepdims=True)
        for board in range(number)
    ]
    sums.append(jnp.zeros((8 - number, trunk.shape[1]), jnp.float32))
    pooled = jnp.concatenate(sums, axis=0) / CELLS
    pass_raw = jnp.sum(pooled * passing[...], axis=1, keepdims=True)
    value = jnp.tanh(jnp.sum(pooled * valuing[...], axis=1, keepdims=True))
    logits = 10.0 * jnp.tanh(raw / 10.0)
    pass_logit = 10.0 * jnp.tanh(pass_raw / 10.0)
    allowed = inside & (legal[...] > 0)
    shares = jnp.sum(jnp.where(allowed, jnp.exp(logits), 0.0), axis=1, keepdims=True)
    scale = jnp.log(shares + jnp.exp(pass_logit))
    padded = jnp.where(allowed, logits - scale, 0.0)
    parts, rest = [], padded
    for _ in range(3):
        parts.append(rest.astype(jnp.bfloat16))
        rest = rest - parts[-1].astype(jnp.float32)
    parts = jnp.concatenate(parts, axis=0)
    moved = jnp.dot(parts, places_of_points[...], preferred_element_type=jnp.float32)
    packed = moved[:8] + moved[8:16] + moved[16:]
    lane = lax.broadcasted_iota(jnp.int32, packed.shape, 1)
    packed = jnp.where(lane == CELLS, pass_logit - scale, packed)
    steps_here, local_count = logp.shape[:2]
    for board in range(number):
        step, local = divmod(board, local_count)
        logp[step, local : local + 1, :] = packed[board : board + 1, : CELLS + 1]
        worth[local : local + 1, step : step + 1] = value[board : board + 1, :]


def run_tower(found, layers, rows, depth, stem, legal, policy, passing, valuing, steps_here, local_count, width):
    number = steps_here * local_count
    point = np.arange(BOARD * width)
    column = point % width
    cell = point // width * BOARD + column % PITCH
    known = (column % PITCH < BOARD) & (column < PITCH * number)
    lanes = -(-(CELLS + 1) // 128) * 128
    target = np.where(known, cell, lanes)[:, None] == np.arange(lanes)[None]
    places_of_points = jnp.asarray(target.astype(jnp.bfloat16))
    points = BOARD * width
    channels = stem.shape[1]
    places = [labels for _, labels in found]
    steps = [0, 5, 10, 15, BOARD]
    cuts = [(low * width, high * width) for low, high in zip(steps, steps[1:])]
    anywhere = pl.BlockSpec(memory_space=pl.ANY)
    inside = pl.BlockSpec(memory_space=pltpu.VMEM)
    return pl.pallas_call(
        functools.partial(tower, places, layers, rows, number, width, cuts),
        out_shape=(
            jax.ShapeDtypeStruct((steps_here, local_count, CELLS + 1), jnp.float32),
            jax.ShapeDtypeStruct((local_count, steps_here), jnp.float32),
        ),
        in_specs=[anywhere] * len(found) + [inside] * 6,
        out_specs=(inside, inside),
        scratch_shapes=[
            pltpu.VMEM((layers, 2, depth, channels), jnp.bfloat16),
            pltpu.VMEM((2, points + 2 * width, 3 * channels), jnp.bfloat16),
            pltpu.VMEM((points, channels), jnp.float32),
            pltpu.VMEM((points, 128), jnp.float32),
            pltpu.VMEM((number, points, 128), jnp.float32),
            pltpu.SemaphoreType.DMA((layers,)),
        ],
        compiler_params=pltpu.CompilerParams(vmem_limit_bytes=36 * 2**20),
        name="tower",
    )(*[block for block, _ in found], stem, legal, policy, passing, valuing, places_of_points)


def padded_boards(rows, width):
    number = rows.shape[0]
    boards = jnp.pad(rows.reshape(number, BOARD, BOARD), ((0, 0), (0, 0), (0, PITCH - BOARD)))
    side_by_side = jnp.swapaxes(boards, 0, 1).reshape(BOARD, number * PITCH)
    return jnp.pad(side_by_side, ((0, 0), (0, width - number * PITCH)))


def stem_stream(boards, sides, stem_weight, width):
    side_move = sides[:, None]
    planes = [boards == 1 + side_move, boards == 2 - side_move, boards == 0, jnp.ones_like(boards)]
    planes = [padded_boards(plane.astype(jnp.bfloat16), width) for plane in planes]
    field = jnp.stack(planes, axis=-1)[None]
    kernel = stem_weight.reshape(3, 3, PLANES, -1)
    out = lax.conv_general_dilated(
        field,
        kernel,
        (1, 1),
        ((1, 1), (1, 1)),
        dimension_numbers=("NHWC", "HWIO", "NHWC"),
        preferred_element_type=jnp.float32,
    )
    return out.reshape(BOARD * width, kernel.shape[-1])


def per_device(
    positions,
    to_move,
    legal_moves,
    master,
    gradients,
    stem_weight,
    policy_weight,
    pass_weight,
    value_weight,
):
    learners, actors = lax.axis_size("learn"), lax.axis_size("act")
    steps_here, local_count = positions.shape[:2]
    number = steps_here * local_count
    width = -(-number * PITCH // 8) * 8
    rows, channels = master.shape[2:]
    depth = rows * actors

    boards = positions.reshape(number, CELLS)
    stem = stem_stream(boards, to_move.reshape(number), stem_weight, width)
    legal = padded_boards(legal_moves.reshape(number, CELLS), width).reshape(1, BOARD * width)

    terms = reduce_gradients(gradients[0], learners, actors)
    *terms, stem, legal = lax.optimization_barrier((*terms, stem, legal))
    updated, rounded = update(terms, master[0], learners)
    found = gather_blocks(rounded, learners, actors)
    if rows % 16:
        whole = jnp.zeros((learners, 2, depth, channels), jnp.bfloat16)
        for block, labels in found:
            for entry, label in enumerate(labels):
                layer, actor = place_of(*label)
                piece = block[2 * entry : 2 * entry + 2]
                whole = lax.dynamic_update_slice(whole, piece[None], (layer, 0, actor * rows, 0))
        found = [(whole, None)]
    logp, values = run_tower(
        found,
        learners,
        rows,
        depth,
        stem,
        legal,
        policy_weight[None],
        pass_weight[None],
        value_weight[None],
        steps_here,
        local_count,
        width,
    )
    return updated[None], logp, values.T


def solution(mesh):
    in_specs = (
        P(None, ("learn", "act"), None),
        P(None, ("learn", "act")),
        P(None, ("learn", "act"), None),
        P("learn", None, "act", None),
        P("learn", None, None, "act", None),
        P(),
        P(),
        P(),
        P(),
    )
    out_specs = (
        P("learn", None, "act", None),
        P(None, ("learn", "act"), None),
        P(None, ("learn", "act")),
    )
    return jax.shard_map(
        per_device, mesh=mesh, in_specs=in_specs, out_specs=out_specs, check_vma=False
    )
```

```python
import functools

import jax
import jax.numpy as jnp
import numpy as np
from jax import lax
from jax.experimental import pallas as pl
from jax.experimental.pallas import tpu as pltpu
from jax.sharding import PartitionSpec as P

BOARD = 19
CELLS = 361
PLANES = 4
PITCH = BOARD + 1
AXES = ("learn", "act")


def pairs(learners, actors, target):
    out = []
    for learner in range(learners):
        for actor in range(actors):
            to_learner, to_actor = target(learner, actor)
            out.append((learner * actors + actor, to_learner * actors + to_actor))
    return out


def route_mask(core, subset, bits):
    mask = 0
    for step in range(bits):
        if subset >> step & 1:
            mask |= 1 << (step if core == 0 else bits - 1 - step)
    return mask


def plane_route(learners, actors, step):
    low, high = 1 << step, learners >> (step + 1)
    return pairs(learners, actors, lambda l, a: (l ^ (low if a % 2 == 0 else high), a))


def pick_kernel(subsets, bits, gradients, *refs):
    outs, arrived = refs[:-1], refs[-1]
    me, core = lax.axis_index("learn"), lax.axis_index("act") % 2
    copies = []
    for number, (subset, out) in enumerate(zip(subsets, outs)):
        layer = me ^ jnp.where(core == 0, route_mask(0, subset, bits), route_mask(1, subset, bits))
        copies.append(pltpu.make_async_copy(gradients.at[layer], out, arrived.at[number]))
        copies[-1].start()
    for copy in copies:
        copy.wait()


def pick(gradients, subsets, bits):
    shape = jax.ShapeDtypeStruct(gradients.shape[1:], gradients.dtype)
    return pl.pallas_call(
        functools.partial(pick_kernel, subsets, bits),
        out_shape=[shape] * len(subsets),
        in_specs=[pl.BlockSpec(memory_space=pl.ANY)],
        out_specs=[pl.BlockSpec(memory_space=pltpu.VMEM)] * len(subsets),
        scratch_shapes=[pltpu.SemaphoreType.DMA((len(subsets),))],
        compiler_params=pltpu.CompilerParams(vmem_limit_bytes=32 * 2**20),
        name="pick",
    )(gradients)


def reduce_gradients(gradients, learners, actors):
    bits = learners.bit_length() - 1
    order = sorted(range(learners), key=lambda subset: (not subset & 1, -subset))
    held, terms = {}, []
    me, core = lax.axis_index("learn"), lax.axis_index("act") % 2
    layer = me ^ jnp.where(core == 0, route_mask(0, order[0], bits), route_mask(1, order[0], bits))
    held[order[0]] = lax.dynamic_index_in_dim(gradients, layer, 0, keepdims=False)
    held.update(zip(order[1:], pick(gradients, order[1:], bits)))
    for step in range(bits):
        route = plane_route(learners, actors, step)
        for subset in sorted(held, reverse=True):
            if subset >> step & 1:
                kept = subset ^ 1 << step
                came = lax.ppermute(held.pop(subset), AXES, route)
                if kept:
                    held[kept] = held[kept] + came
                else:
                    terms.append(came)
    return held[0], *terms


def update_kernel(learners, *refs):
    *terms, master, updated, rounded = refs
    total = terms[0][...]
    for term in terms[1:]:
        total = total + term[...]
    new = master[...] - total / learners
    updated[...] = new
    rounded[...] = new.astype(jnp.bfloat16)


def update(terms, master, learners):
    inside = pl.BlockSpec(memory_space=pltpu.VMEM)
    return pl.pallas_call(
        functools.partial(update_kernel, learners),
        out_shape=(
            jax.ShapeDtypeStruct(master.shape, jnp.float32),
            jax.ShapeDtypeStruct(master.shape, jnp.bfloat16),
        ),
        in_specs=[inside] * (len(terms) + 1),
        out_specs=(inside, inside),
        compiler_params=pltpu.CompilerParams(vmem_limit_bytes=32 * 2**20),
        name="update",
    )(*terms, master)


def gather_blocks(own, learners, actors):
    bits = learners.bit_length() - 1
    chips = actors // 2

    def along_z(block, away):
        return lax.ppermute(block, AXES, pairs(learners, actors, lambda l, a: (l, a ^ (2 * away))))

    def along_plane(block, step):
        return lax.ppermute(block, AXES, plane_route(learners, actors, step))

    def swapped(block):
        return lax.ppermute(block, AXES, pairs(learners, actors, lambda l, a: (l, a ^ 1)))

    def label(away, subset):
        masks = (route_mask(0, subset, bits), route_mask(1, subset, bits))
        return masks, 2 * away

    def other_label(away, subset):
        masks, actor_mask = label(away, subset)
        return masks[::-1], actor_mask + 1

    found = []
    starts = {0: own}
    for away in range(1, chips):
        starts[away] = along_z(starts[away - 1], 1) if away % 2 and away > 1 else along_z(own, away)
    for away in range(chips):
        held = {0: starts[away]}
        for step in range(bits):
            for subset in sorted(held):
                if (away, subset | 1 << step) in ((1,3),):
                    held[subset | 1 << step] = along_z(before[subset | 1 << step], 1)
                else:
                    held[subset | 1 << step] = along_plane(held[subset], step)
        before = held
        groups = [sorted(held)] if away < chips - 1 else [sorted(held)[:-1], [learners - 1]]
        for group in groups:
            joined = jnp.concatenate([held[subset] for subset in group], axis=0) if len(group) > 1 else held[group[0]]
            found.append((swapped(joined), [other_label(away, subset) for subset in group]))
        found.extend((held[subset], [label(away, subset)]) for subset in sorted(held))
    return found


def place_of(masks, actor_mask):
    actor = lax.axis_index("act")
    mask = jnp.where(actor % 2 == 0, masks[0], masks[1])
    return lax.axis_index("learn") ^ mask, actor ^ actor_mask


def tower(places, layers, rows, number, width, cuts, *refs):
    blocks = refs[: len(places)]
    stem, legal, policy, passing, valuing, places_of_points, mask, of_board, owned, logp, worth = refs[len(places) : len(places) + 11]
    weights, field, stream, arrived = refs[len(places) + 11 :]
    points = BOARD * width
    for labels, block in zip(places, blocks):
        if labels is None:
            for layer in range(layers):
                pltpu.make_async_copy(block.at[layer], weights.at[layer], arrived.at[layer]).start()
            continue
        for entry, label in enumerate(labels):
            layer, actor = place_of(*label)
            spot = pl.ds(pl.multiple_of(actor * rows, rows), rows)
            pltpu.make_async_copy(
                block.at[2 * entry : 2 * entry + 2], weights.at[layer, :, spot, :], arrived.at[layer]
            ).start()
    for half in range(2):
        field[half, :width, :] = jnp.zeros((width, field.shape[2]), jnp.bfloat16)
        field[half, width + points :, :] = jnp.zeros((width, field.shape[2]), jnp.bfloat16)

    def rectified(low, high, values):
        keep = mask[low:high, :]
        keep = jnp.concatenate([keep] * (values.shape[1] // keep.shape[1]), axis=1)
        return jnp.maximum(values, 0.0) * keep

    def spread(half, low, high, values):
        values = rectified(low, high, values)
        depth = values.shape[1]
        spot = slice(width + low, width + high)
        field[half, spot, depth : 2 * depth] = values.astype(jnp.bfloat16)
        field[half, spot, :depth] = pltpu.roll(values, 1, 0).astype(jnp.bfloat16)
        field[half, spot, 2 * depth :] = pltpu.roll(values, high - low - 1, 0).astype(jnp.bfloat16)

    def convolve(half, layer, which, low, high):
        lines = [field[half, low + row * width : high + row * width, :] for row in range(3)]
        return jnp.dot(
            jnp.concatenate(lines, axis=1), weights[layer, which], preferred_element_type=jnp.float32
        )

    for low, high in cuts:
        values = stem[low:high, :]
        stream[low:high, :] = values
        spread(0, low, high, values)
    for layer in range(layers):
        pltpu.make_async_copy(weights.at[layer], weights.at[layer], arrived.at[layer]).wait()
        for low, high in cuts:
            spread(1, low, high, convolve(0, layer, 0, low, high))
        for low, high in cuts:
            values = stream[low:high, :] + convolve(1, layer, 1, low, high)
            if layer == layers - 1:
                stream[low:high, :] = rectified(low, high, values)
            else:
                stream[low:high, :] = values
                spread(0, low, high, values)

    trunk = stream[...]
    inside = owned[...] > 0
    exact = functools.partial(
        lax.dot_general, precision=lax.Precision.HIGHEST, preferred_element_type=jnp.float32
    )
    weighted = trunk * policy[...]
    weighted = sum(weighted[:, part : part + 128] for part in range(0, weighted.shape[1], 128))
    raw = exact(jnp.ones((8, 128), jnp.float32), weighted, (((1,), (1,)), ((), ())))
    sums = [
        jnp.sum(trunk * jnp.concatenate([of_board[board]] * (trunk.shape[1] // 128), axis=1), axis=0, keepdims=True)
        for board in range(number)
    ]
    sums.append(jnp.zeros((8 - number, trunk.shape[1]), jnp.float32))
    pooled = jnp.concatenate(sums, axis=0) / CELLS
    pass_raw = jnp.sum(pooled * passing[...], axis=1, keepdims=True)
    value = jnp.tanh(jnp.sum(pooled * valuing[...], axis=1, keepdims=True))
    logits = 10.0 * jnp.tanh(raw / 10.0)
    pass_logit = 10.0 * jnp.tanh(pass_raw / 10.0)
    allowed = inside & (legal[...] > 0)
    shares = jnp.sum(jnp.where(allowed, jnp.exp(logits), 0.0), axis=1, keepdims=True)
    scale = jnp.log(shares + jnp.exp(pass_logit))
    padded = jnp.where(allowed, logits - scale, 0.0)
    parts, rest = [], padded
    for _ in range(3):
        parts.append(rest.astype(jnp.bfloat16))
        rest = rest - parts[-1].astype(jnp.float32)
    parts = jnp.concatenate(parts, axis=0)
    moved = jnp.dot(parts, places_of_points[...], preferred_element_type=jnp.float32)
    packed = moved[:8] + moved[8:16] + moved[16:]
    lane = lax.broadcasted_iota(jnp.int32, packed.shape, 1)
    packed = jnp.where(lane == CELLS, pass_logit - scale, packed)
    steps_here, local_count = logp.shape[:2]
    for board in range(number):
        step, local = divmod(board, local_count)
        logp[step, local : local + 1, :] = packed[board : board + 1, : CELLS + 1]
        worth[local : local + 1, step : step + 1] = value[board : board + 1, :]


def run_tower(found, layers, rows, depth, stem, legal, policy, passing, valuing, steps_here, local_count, width):
    number = steps_here * local_count
    point = np.arange(BOARD * width)
    column = point % width
    cell = point // width * BOARD + column % PITCH
    known = (column % PITCH < BOARD) & (column < PITCH * number)
    lanes = -(-(CELLS + 1) // 128) * 128
    target = np.where(known, cell, lanes)[:, None] == np.arange(lanes)[None]
    places_of_points = jnp.asarray(target.astype(jnp.bfloat16))
    owner = np.where(known, column // PITCH, -1)
    mask = jnp.asarray(np.repeat(known[:, None], 128, axis=1).astype(np.float32))
    of_board = np.arange(number)[:, None] == owner[None]
    of_board = jnp.asarray(np.repeat(of_board[:, :, None], 128, axis=2).astype(np.float32))
    owned = jnp.asarray((np.arange(8)[:, None] == owner[None]).astype(np.float32))
    points = BOARD * width
    channels = stem.shape[1]
    places = [labels for _, labels in found]
    steps = [0, 5, 10, 15, BOARD]
    cuts = [(low * width, high * width) for low, high in zip(steps, steps[1:])]
    anywhere = pl.BlockSpec(memory_space=pl.ANY)
    inside = pl.BlockSpec(memory_space=pltpu.VMEM)
    return pl.pallas_call(
        functools.partial(tower, places, layers, rows, number, width, cuts),
        out_shape=(
            jax.ShapeDtypeStruct((steps_here, local_count, CELLS + 1), jnp.float32),
            jax.ShapeDtypeStruct((local_count, steps_here), jnp.float32),
        ),
        in_specs=[anywhere] * len(found) + [inside] * 9,
        out_specs=(inside, inside),
        scratch_shapes=[
            pltpu.VMEM((layers, 2, depth, channels), jnp.bfloat16),
            pltpu.VMEM((2, points + 2 * width, 3 * channels), jnp.bfloat16),
            pltpu.VMEM((points, channels), jnp.float32),
            pltpu.SemaphoreType.DMA((layers,)),
        ],
        compiler_params=pltpu.CompilerParams(vmem_limit_bytes=36 * 2**20),
        name="tower",
    )(*[block for block, _ in found], stem, legal, policy, passing, valuing, places_of_points, mask, of_board, owned)


def padded_boards(rows, width):
    number = rows.shape[0]
    boards = jnp.pad(rows.reshape(number, BOARD, BOARD), ((0, 0), (0, 0), (0, PITCH - BOARD)))
    side_by_side = jnp.swapaxes(boards, 0, 1).reshape(BOARD, number * PITCH)
    return jnp.pad(side_by_side, ((0, 0), (0, width - number * PITCH)))


def stem_stream(boards, sides, stem_weight, width):
    side_move = sides[:, None]
    planes = [boards == 1 + side_move, boards == 2 - side_move, boards == 0, jnp.ones_like(boards)]
    planes = [padded_boards(plane.astype(jnp.bfloat16), width) for plane in planes]
    field = jnp.stack(planes, axis=-1)[None]
    kernel = stem_weight.reshape(3, 3, PLANES, -1)
    out = lax.conv_general_dilated(
        field,
        kernel,
        (1, 1),
        ((1, 1), (1, 1)),
        dimension_numbers=("NHWC", "HWIO", "NHWC"),
        preferred_element_type=jnp.float32,
    )
    return out.reshape(BOARD * width, kernel.shape[-1])


def per_device(
    positions,
    to_move,
    legal_moves,
    master,
    gradients,
    stem_weight,
    policy_weight,
    pass_weight,
    value_weight,
):
    learners, actors = lax.axis_size("learn"), lax.axis_size("act")
    steps_here, local_count = positions.shape[:2]
    number = steps_here * local_count
    width = -(-number * PITCH // 8) * 8
    rows, channels = master.shape[2:]
    depth = rows * actors

    boards = positions.reshape(number, CELLS)
    stem = stem_stream(boards, to_move.reshape(number), stem_weight, width)
    legal = padded_boards(legal_moves.reshape(number, CELLS), width).reshape(1, BOARD * width)

    terms = reduce_gradients(gradients[0], learners, actors)
    *terms, stem, legal = lax.optimization_barrier((*terms, stem, legal))
    updated, rounded = update(terms, master[0], learners)
    found = gather_blocks(rounded, learners, actors)
    if rows % 16:
        whole = jnp.zeros((learners, 2, depth, channels), jnp.bfloat16)
        for block, labels in found:
            for entry, label in enumerate(labels):
                layer, actor = place_of(*label)
                piece = block[2 * entry : 2 * entry + 2]
                whole = lax.dynamic_update_slice(whole, piece[None], (layer, 0, actor * rows, 0))
        found = [(whole, None)]
    logp, values = run_tower(
        found,
        learners,
        rows,
        depth,
        stem,
        legal,
        policy_weight[None],
        pass_weight[None],
        value_weight[None],
        steps_here,
        local_count,
        width,
    )
    return updated[None], logp, values.T


def solution(mesh):
    in_specs = (
        P(None, ("learn", "act"), None),
        P(None, ("learn", "act")),
        P(None, ("learn", "act"), None),
        P("learn", None, "act", None),
        P("learn", None, None, "act", None),
        P(),
        P(),
        P(),
        P(),
    )
    out_specs = (
        P("learn", None, "act", None),
        P(None, ("learn", "act"), None),
        P(None, ("learn", "act")),
    )
    return jax.shard_map(
        per_device, mesh=mesh, in_specs=in_specs, out_specs=out_specs, check_vma=False
    )
```
